512 devices in a mesh: row: 16 (over y_lo, x), col: 32 (over z, y_hi, core).
Axes of the slice: x: 4, y: 8 (y_hi: 2, y_lo: 4; y = y_hi * 4 + y_lo), z: 8, core: 2. Of those that a mesh axis runs over, the one named last changes fastest.
Arguments:
- gradient: bfloat16 [8192, 28672], P('row', 'col'), may hold values from -6 to 6
- projector: bfloat16 [8192, 1024], P(('row', 'col')), may hold values from -0.25 to 0.25
- first_moment: float32 [1024, 28672], P('row', 'col'), may hold values from -3 to 3
- second_moment: float32 [1024, 28672], P('row', 'col'), may hold values from 0.01 to 1
Outputs:
- update: float32 [8192, 28672], P('row', 'col')
- first_new: float32 [1024, 28672], P('row', 'col')
- second_new: float32 [1024, 28672], P('row', 'col')
The draws below stay inside these ranges and needn't reach their ends.
All inputs are finite; a program needn't handle non-finite values.
Results may differ from the reference program's by a relative error of at most 0.0029.
Values may be sent and summed in bfloat16 or wider, within the bound.
A program may use at most 64 MiB of HBM per device.

```python
import math
import jax
import jax.numpy as jnp

D = 8192
FF = 28672
RANK = 1024


def spiked(array, key, source, target, parts, factor):
    owner, partner = [(jnp.arange(array.shape[dim]) // (array.shape[dim] // parts)).reshape([-1 if axis == dim else 1 for axis in range(array.ndim)]) for dim in (source, target)]
    chosen = jax.random.permutation(key, parts)[partner]
    strong = (owner == chosen) | (owner == (partner + parts // 2) % parts)
    return jnp.where(strong, factor * array, array)


def level_of(key, dims, pieces, least, top_value):
    level, own = 1.0, jax.random.fold_in(key, 6)
    for dim, shards_of in pieces:
        steps = jnp.exp(jax.random.uniform(jax.random.fold_in(own, dim), (shards_of,), jnp.float32, least / len(pieces), top_value / len(pieces)))
        level = level * jnp.repeat(steps, dims[dim] // shards_of).reshape([-1 if axis == dim else 1 for axis in range(len(dims))])
    return level


def bell_draw(own_key, dims, scale, most, pieces=(), dtype=jnp.bfloat16):
    drawn = jax.random.normal(own_key, dims, jnp.float32) * scale
    if len(pieces) > 0:
        drawn = level_of(own_key, dims, pieces, -0.22, 0.18) * drawn
    return jnp.clip(drawn, min=-most, max=most).astype(dtype)


def bell_draw_with(own_key, dims, scale, reach, shards, heavy, kind=jnp.bfloat16):
    drawn = scale * jax.random.normal(own_key, dims, jnp.float32)
    if shards:
        drawn = drawn * level_of(own_key, dims, shards, -0.22, 0.18)
    return jnp.clip(spiked(drawn, jax.random.fold_in(own_key, 3), *heavy), -reach, reach).astype(kind)


def setup_inputs(seed: int = 0) -> dict:
    seeds = jax.random.split(jax.random.key(seed), 5)
    return {
        "gradient": bell_draw(seeds[0], (D, FF), 1.0, 6.0, ((0, 16), (1, 32))),
        "projector": bell_draw_with(seeds[1], (D, RANK), D ** -0.5, 0.25, ((0, 512),), (0, 1, 512, 6.0)),
        "first_moment": bell_draw(seeds[2], (RANK, FF), 0.3, 3.0, ((0, 16), (1, 32)), jnp.float32),
        "second_moment": jnp.clip(jnp.exp(math.log(1.0) - 4.6051702 * jax.random.uniform(seeds[3], (RANK, FF), jnp.float32) ** level_of(seeds[3], (RANK, FF), ((0, 16), (1, 32)), -0.2, 0.2)), 0.01, 1.0),
    }


beta_first = 0.9
beta_second = 0.999
epsilon = 1e-08

def reference(gradient, projector, first_moment, second_moment):
    lowrank = jnp.dot(projector.T, gradient, preferred_element_type=jnp.float32)
    first_new = beta_first * first_moment + (1.0 - beta_first) * lowrank
    second_new = beta_second * second_moment + (1.0 - beta_second) * lowrank * lowrank
    direction = (first_new / (jnp.sqrt(second_new) + epsilon)).astype(jnp.bfloat16)
    update = jnp.dot(projector, direction, preferred_element_type=jnp.float32)
    return (update, first_new, second_new)
```

```python
import jax
import jax.numpy as jnp
from jax import lax
from jax.experimental import pallas as pl
from jax.experimental.pallas import tpu as pltpu
from jax.sharding import PartitionSpec as P

MESH = pl.DeviceIdType.MESH
beta_first = 0.9
beta_second = 0.999
epsilon = 1e-08

NX, NY, NZ = 4, 4, 8
CHUNK = 256
OWN = 64
COLS = 896
ROWS = 512


def kernel(
    grad, proj, mom1, mom2, update, first, second,
    pg, part, xs, xr, ys, yr, dirs,
    local_sem, ps_send, ps_recv, pf_send, pf_recv, sw_send, sw_recv,
    xs_sem, xr_sem, ys_sem, yr_sem, dx_send, dx_recv, dy_send, dy_recv,
):
    row = lax.axis_index("row")
    col = lax.axis_index("col")
    x, y = lax.rem(row, NX), lax.div(row, NX)
    k, h, z = lax.rem(col, 2), lax.rem(lax.div(col, 2), 2), lax.div(col, 4)
    zh = z * 2 + h

    def at_zh(dz, flip):
        other_z = lax.rem(z + dz, NZ)
        other_h = lax.rem(h + flip, 2)
        return (row, (other_z * 2 + other_h) * 2 + k)

    def at_x(d):
        return (y * NX + lax.rem(x + d, NX), col)

    def at_y(e):
        return (lax.rem(y + e, NY) * NX + x, col)

    other_core = (row, zh * 2 + 1 - k)

    def own_chunk(j):
        c = lax.rem(y + 1 + j, NY)
        return pltpu.make_async_copy(
            proj.at[:, pl.ds(pl.multiple_of(c * CHUNK, CHUNK), CHUNK)], pg.at[j, zh, k], local_sem.at[j]
        )

    for j in range(NY):
        own_chunk(j).start()

    barrier = pltpu.get_barrier_semaphore()

    @pl.loop(1, 16)
    def _(i):
        pl.semaphore_signal(barrier, inc=1, device_id=at_zh(lax.div(i, 2), lax.rem(i, 2)), device_id_type=MESH)

    @pl.loop(1, 4)
    def _(i):
        pl.semaphore_signal(barrier, inc=1, device_id=at_x(i), device_id_type=MESH)
        pl.semaphore_signal(barrier, inc=1, device_id=at_y(i), device_id_type=MESH)

    pl.semaphore_signal(barrier, inc=1, device_id=other_core, device_id_type=MESH)
    for j in range(NY):
        own_chunk(j).wait()
    pl.semaphore_wait(barrier, 22)

    def send_first(i):
        return pltpu.make_async_remote_copy(
            src_ref=pg.at[0, zh, k], dst_ref=pg.at[0, zh, k], send_sem=ps_send.at[i], recv_sem=ps_recv.at[i],
            device_id=at_zh(lax.div(i, 2), lax.rem(i, 2)), device_id_type=MESH)

    @pl.loop(0, 15)
    def _(i):
        send_first(15 - i).start()

    def send_rest(i, from_half):
        piece = pg.at[pl.ds(1, 3), z * 2 + lax.rem(h + from_half, 2), k]
        return pltpu.make_async_remote_copy(
            src_ref=piece, dst_ref=piece, send_sem=pf_send.at[from_half, i], recv_sem=pf_recv.at[from_half, i],
            device_id=at_zh(i, 0), device_id_type=MESH)

    def send_half():
        piece = pg.at[pl.ds(1, 3), zh, k]
        return pltpu.make_async_remote_copy(
            src_ref=piece, dst_ref=piece, send_sem=pf_send.at[0, 0], recv_sem=pf_recv.at[0, 0],
            device_id=at_zh(0, 1), device_id_type=MESH)

    send_half().start()

    @pl.loop(1, NZ)
    def _(i):
        send_rest(i, 0).start()

    def swap(first_chunk, count, s):
        piece = pg.at[pl.ds(first_chunk, count), :, k]
        return pltpu.make_async_remote_copy(
            src_ref=piece, dst_ref=piece, send_sem=sw_send.at[s], recv_sem=sw_recv.at[s],
            device_id=other_core, device_id_type=MESH)

    @pl.loop(1, 16)
    def _(i):
        send_first(i).wait_recv()

    swap(0, 1, 0).start()
    send_half().wait_recv()

    @pl.loop(1, NZ)
    def _(i):
        send_rest(i, 1).start()

    swap(0, 1, 0).wait_recv()

    def send_x(j, d):
        return pltpu.make_async_remote_copy(
            src_ref=xs.at[j, lax.rem(x + d, NX)], dst_ref=xr.at[j, d - 1], send_sem=xs_sem.at[j, d - 1],
            recv_sem=xr_sem.at[j, d - 1], device_id=at_x(d), device_id_type=MESH)

    def project(j):
        sums = lax.dot_general(
            pg[j].reshape(ROWS, CHUNK), grad[...], (((0,), (0,)), ((), ())), preferred_element_type=jnp.float32)
        sums = sums.reshape(NX, OWN, COLS)
        part[j] = sums
        xs[j] = sums.astype(jnp.bfloat16)
        for d in (2, 1, 3):
            send_x(j, d).start()

    def send_y(j):
        return pltpu.make_async_remote_copy(
            src_ref=ys.at[j], dst_ref=yr.at[j], send_sem=ys_sem.at[j], recv_sem=yr_sem.at[j],
            device_id=at_y(j + 1), device_id_type=MESH)

    def sum_x(j):
        total = part[j, x]
        for d in (1, 3, 2):
            send_x(j, d).wait_recv()
            total += xr[j, d - 1].astype(jnp.float32)
        return total

    project(0)

    @pl.loop(1, NZ)
    def _(i):
        send_rest(i, 0).wait_recv()
        send_rest(i, 1).wait_recv()

    swap(1, 3, 1).start()
    swap(1, 3, 1).wait_recv()

    @pl.loop(1, NY)
    def _(j):
        project(j)
        ys[j - 1] = sum_x(j - 1).astype(jnp.bfloat16)
        send_y(j - 1).start()

    lowrank = sum_x(3)
    for j in range(3):
        send_y(j).wait_recv()
        lowrank += yr[j].astype(jnp.float32)

    first_new = beta_first * mom1[...] + (1.0 - beta_first) * lowrank
    second_new = beta_second * mom2[...] + (1.0 - beta_second) * lowrank * lowrank
    dirs[3, x] = (first_new / (jnp.sqrt(second_new) + epsilon)).astype(jnp.bfloat16)

    def dir_y(e):
        return pltpu.make_async_remote_copy(
            src_ref=dirs.at[3, x], dst_ref=dirs.at[3 - e, x], send_sem=dy_send.at[e - 1], recv_sem=dy_recv.at[e - 1],
            device_id=at_y(e), device_id_type=MESH)

    def dir_x(s, d):
        return pltpu.make_async_remote_copy(
            src_ref=dirs.at[s, x], dst_ref=dirs.at[s, x], send_sem=dx_send.at[s, d - 1], recv_sem=dx_recv.at[s, d - 1],
            device_id=at_x(d), device_id_type=MESH)

    for e in (2, 1, 3):
        dir_y(e).start()
    for d in (2, 1, 3):
        dir_x(3, d).start()
    first[...] = first_new
    second[...] = second_new

    for e in (1, 3, 2):
        dir_y(e).wait_recv()
        for d in (2, 1, 3):
            dir_x(3 - e, d).start()

    def expand(s):
        for d in (1, 3, 2):
            dir_x(s, d).wait_recv()
        return jnp.dot(pg[s].reshape(ROWS, CHUNK), dirs[s].reshape(CHUNK, COLS), preferred_element_type=jnp.float32)

    update[...] = expand(3)
    for s in (2, 0, 1):
        update[...] += expand(s)

    @pl.loop(1, 16)
    def _(i):
        send_first(i).wait_send()

    send_half().wait_send()

    @pl.loop(1, NZ)
    def _(i):
        send_rest(i, 0).wait_send()
        send_rest(i, 1).wait_send()

    swap(0, 1, 0).wait_send()
    swap(1, 3, 1).wait_send()
    for d in (1, 2, 3):
        send_y(d - 1).wait_send()
        dir_y(d).wait_send()

        @pl.loop(0, NY)
        def _(j):
            send_x(j, d).wait_send()
            dir_x(j, d).wait_send()


def on_device(gradient, projector, first_moment, second_moment):
    vmem = pl.BlockSpec(memory_space=pltpu.VMEM)
    dma = pltpu.SemaphoreType.DMA
    return pl.pallas_call(
        kernel,
        out_shape=(
            jax.ShapeDtypeStruct((ROWS, COLS), jnp.float32),
            jax.ShapeDtypeStruct((OWN, COLS), jnp.float32),
            jax.ShapeDtypeStruct((OWN, COLS), jnp.float32),
        ),
        in_specs=[vmem, vmem, vmem, vmem],
        out_specs=(vmem, vmem, vmem),
        scratch_shapes=[
            pltpu.VMEM((NY, 16, 2, 16, CHUNK), jnp.bfloat16),
            pltpu.VMEM((NY, NX, OWN, COLS), jnp.float32),
            pltpu.VMEM((NY, NX, OWN, COLS), jnp.bfloat16),
            pltpu.VMEM((NY, 3, OWN, COLS), jnp.bfloat16),
            pltpu.VMEM((3, OWN, COLS), jnp.bfloat16),
            pltpu.VMEM((3, OWN, COLS), jnp.bfloat16),
            pltpu.VMEM((NY, NX, OWN, COLS), jnp.bfloat16),
            dma((4,)),
            dma((16,)), dma((16,)),
            dma((2, NZ)), dma((2, NZ)),
            dma((2,)), dma((2,)),
            dma((4, 3)), dma((4, 3)),
            dma((3,)), dma((3,)),
            dma((4, 3)), dma((4, 3)),
            dma((3,)), dma((3,)),
        ],
        compiler_params=pltpu.CompilerParams(
            collective_id=0, has_side_effects=True, vmem_limit_bytes=48 * 1024 * 1024
        ),
        cost_estimate=pl.CostEstimate(flops=4 * 512 * 1024 * 896, bytes_accessed=4 << 20, transcendentals=0),
    )(gradient, projector, first_moment, second_moment)


def solution(mesh):
    return jax.shard_map(
        on_device,
        mesh=mesh,
        in_specs=(P("row", "col"), P(("row", "col"), None), P("row", "col"), P("row", "col")),
        out_specs=(P("row", "col"), P("row", "col"), P("row", "col")),
        check_vma=False,
    )
```

```python
import jax
import jax.numpy as jnp
from jax import lax
from jax.experimental import pallas as pl
from jax.experimental.pallas import tpu as pltpu
from jax.sharding import PartitionSpec as P

MESH = pl.DeviceIdType.MESH
beta_first = 0.9
beta_second = 0.999
epsilon = 1e-08

NX, NY, NZ = 4, 4, 8
CHUNK = 256
OWN = 64
PART = 32
HALF = 16
COLS = 896
ROWS = 512


def kernel(
    grad_hbm, proj_hbm, mom1_hbm, mom2_hbm, update, first, second,
    grad, proj, mom1, mom2, pg, part, xs, ss, xr, ys, yr, dirs,
    local_sem, ps_send, ps_recv, hf_send, hf_recv, pf_send, pf_recv, sw_send, sw_recv,
    xs_sem, xr_sem, ys_sem, yr_sem, dx_send, dx_recv, dy_send, dy_recv,
):
    row = lax.axis_index("row")
    col = lax.axis_index("col")
    x, y = lax.rem(row, NX), lax.div(row, NX)
    k, h, z = lax.rem(col, 2), lax.rem(lax.div(col, 2), 2), lax.div(col, 4)
    zh = z * 2 + h

    def at_zh(dz, flip):
        other_z = lax.rem(z + dz, NZ)
        other_h = lax.rem(h + flip, 2)
        return (row, (other_z * 2 + other_h) * 2 + k)

    def x_of(d):
        return lax.rem(x + d, NX)

    def at_x(d):
        return (y * NX + x_of(d), col)

    def y_of(t):
        return lax.rem(lax.div(y, 2) + t // 2, 2) * 2 + lax.rem(lax.rem(y, 2) + t % 2, 2)

    def at_y(t):
        return (y_of(t) * NX + x, col)

    def remote(src, dst, send_sem, recv_sem, device):
        return pltpu.make_async_remote_copy(
            src_ref=src, dst_ref=dst, send_sem=send_sem, recv_sem=recv_sem, device_id=device, device_id_type=MESH)

    other_core = (row, zh * 2 + 1 - k)

    fetch_proj = pltpu.make_async_copy(proj_hbm, proj, local_sem.at[0])
    fetch_grad = pltpu.make_async_copy(grad_hbm, grad, local_sem.at[1])
    fetch_mom1 = pltpu.make_async_copy(mom1_hbm, mom1, local_sem.at[2])
    fetch_mom2 = pltpu.make_async_copy(mom2_hbm, mom2, local_sem.at[3])
    fetch_proj.start()

    barrier = pltpu.get_barrier_semaphore()

    @pl.loop(1, 16)
    def _(i):
        pl.semaphore_signal(barrier, inc=1, device_id=at_zh(lax.div(i, 2), lax.rem(i, 2)), device_id_type=MESH)

    for t in (1, 2, 3):
        pl.semaphore_signal(barrier, inc=1, device_id=at_y(t), device_id_type=MESH)
    for d in (1, 3):
        pl.semaphore_signal(barrier, inc=1, device_id=at_x(d), device_id_type=MESH)
    pl.semaphore_signal(barrier, inc=1, device_id=other_core, device_id_type=MESH)

    fetch_grad.start()
    fetch_mom1.start()
    fetch_mom2.start()
    fetch_proj.wait()

    for j in range(NY):
        owned = proj[:, pl.ds(pl.multiple_of(y_of(3 - j) * CHUNK, CHUNK), CHUNK)]
        for half in range(2):
            s = 4 * half + j
            picked = [owned[:, OWN * i + PART * half : OWN * i + PART * (half + 1)] for i in range(NX)]
            pg[s // 2, zh, k, :, pl.ds(s % 2 * 128, 128)] = jnp.concatenate(picked, axis=1)
    pl.semaphore_wait(barrier, 21)

    def send_first(i):
        piece = pg.at[0, zh, k]
        return remote(piece, piece, ps_send.at[i], ps_recv.at[i], at_zh(lax.div(i, 2), lax.rem(i, 2)))

    @pl.loop(0, 15)
    def _(i):
        send_first(15 - i).start()

    def send_half():
        piece = pg.at[pl.ds(1, 3), zh, k]
        return remote(piece, piece, hf_send, hf_recv, at_zh(0, 1))

    def send_rest(g, i, from_half):
        piece = pg.at[g, z * 2 + lax.rem(h + from_half, 2), k]
        return remote(piece, piece, pf_send.at[g - 1, from_half, i], pf_recv.at[g - 1, from_half, i], at_zh(i, 0))

    def send_rests(g, from_half):
        @pl.loop(1, NZ)
        def _(i):
            send_rest(g, lax.rem(i + 3, NZ - 1) + 1, from_half).start()

    def swap(g):
        piece = pg.at[g, :, k]
        return remote(piece, piece, sw_send.at[g], sw_recv.at[g], other_core)

    send_half().start()
    send_rests(1, 0)
    send_half().wait_recv()
    send_rests(1, 1)

    @pl.loop(1, 16)
    def _(i):
        send_first(i).wait_recv()

    swap(0).start()
    for g in (2, 3):
        send_rests(g, 0)
        send_rests(g, 1)
    fetch_grad.wait()
    swap(0).wait_recv()

    def rest_here(g):
        @pl.loop(1, NZ)
        def _(i):
            send_rest(g, i, 0).wait_recv()
            send_rest(g, i, 1).wait_recv()

        swap(g).start()

    low, high = pl.ds(0, HALF), pl.ds(HALF, HALF)

    def send_x(s, kind):
        src, d = (
            (xs.at[s, x_of(2), low], 1),
            (xs.at[s, x_of(2), high], 3),
            (xs.at[s, x_of(1), high], 1),
            (xs.at[s, x_of(3), low], 3),
            (ss.at[s, 0], 1),
            (ss.at[s, 1], 3),
        )[kind]
        return remote(src, xr.at[s, kind], xs_sem.at[s, kind], xr_sem.at[s, kind], at_x(d))

    def project(q):
        sums = lax.dot_general(
            pg[q].reshape(ROWS, CHUNK), grad[...], (((0,), (0,)), ((), ())), preferred_element_type=jnp.float32)
        sums = sums.reshape(2, NX, PART, COLS)
        part[pl.ds(2 * q, 2)] = sums
        xs[pl.ds(2 * q, 2)] = sums.astype(jnp.bfloat16)
        for kinds in ((0, 1), (2, 3)):
            for s in (2 * q, 2 * q + 1):
                for kind in kinds:
                    send_x(s, kind).start()

    def relay(s):
        send_x(s, 0).wait_recv()
        ss[s, 0] = (part[s, x_of(1), low] + xr[s, 0].astype(jnp.float32)).astype(jnp.bfloat16)
        send_x(s, 4).start()
        send_x(s, 1).wait_recv()
        ss[s, 1] = (part[s, x_of(3), high] + xr[s, 1].astype(jnp.float32)).astype(jnp.bfloat16)
        send_x(s, 5).start()

    def sum_x(s):
        for kind in range(2, 6):
            send_x(s, kind).wait_recv()
        lower = part[s, x, low] + xr[s, 3].astype(jnp.float32) + xr[s, 4].astype(jnp.float32)
        upper = part[s, x, high] + xr[s, 2].astype(jnp.float32) + xr[s, 5].astype(jnp.float32)
        return jnp.concatenate([lower, upper], axis=0)

    def send_y(s):
        return remote(ys.at[s], yr.at[s], ys_sem.at[s], yr_sem.at[s], at_y(3 - s % 4))

    def finish(s):
        ys[s] = sum_x(s).astype(jnp.bfloat16)
        send_y(s).start()

    def dir_y(half, t):
        own = 4 * half + 3
        return remote(dirs.at[own, x], dirs.at[own - t, x], dy_send.at[half, t - 1], dy_recv.at[half, t - 1], at_y(t))

    def dir_x(s, kind):
        src, d = (
            (dirs.at[s, x], 1),
            (dirs.at[s, x], 3),
            (dirs.at[s, x_of(3), low], 1),
            (dirs.at[s, x_of(1), high], 3),
        )[kind]
        return remote(src, src, dx_send.at[s, kind], dx_recv.at[s, kind], at_x(d))

    def spread(s):
        dir_x(s, 0).start()
        dir_x(s, 1).start()

    def spread_here(half, t):
        dir_y(half, t).wait_recv()
        spread(4 * half + 3 - t)

    def forward(s):
        for kind in range(2):
            dir_x(s, kind).wait_recv()
            dir_x(s, kind + 2).start()

    def expand(q):
        for s in (2 * q, 2 * q + 1):
            for kind in range(2, 4):
                dir_x(s, kind).wait_recv()
        return jnp.dot(
            pg[q].reshape(ROWS, CHUNK), dirs[pl.ds(2 * q, 2)].reshape(CHUNK, COLS), preferred_element_type=jnp.float32)

    def step(half):
        own = 4 * half + 3
        rows = pl.ds(PART * half, PART)
        lowrank = sum_x(own)
        for j in range(3):
            send_y(4 * half + j).wait_recv()
            lowrank += yr[4 * half + j].astype(jnp.float32)
        first_new = beta_first * mom1[rows] + (1.0 - beta_first) * lowrank
        second_new = beta_second * mom2[rows] + (1.0 - beta_second) * lowrank * lowrank
        dirs[own, x] = (first_new / (jnp.sqrt(second_new) + epsilon)).astype(jnp.bfloat16)
        for t in (3, 2, 1):
            dir_y(half, t).start()
        spread(own)
        first[rows] = first_new
        second[rows] = second_new

    project(0)
    rest_here(1)
    relay(0)
    relay(1)
    swap(1).wait_recv()
    project(1)
    rest_here(2)
    finish(0)
    finish(1)
    swap(2).wait_recv()
    relay(2)
    relay(3)
    project(2)
    rest_here(3)
    swap(3).wait_recv()
    project(3)
    finish(2)
    relay(4)
    relay(5)
    fetch_mom1.wait()
    fetch_mom2.wait()
    step(0)
    relay(6)
    relay(7)
    finish(4)
    finish(5)
    finish(6)
    spread_here(0, 1)
    forward(3)
    spread_here(0, 2)
    forward(2)
    step(1)
    spread_here(0, 3)
    forward(1)
    forward(0)
    update[...] = expand(1)

    @pl.loop(1, 16)
    def _(i):
        send_first(i).wait_send()

    send_half().wait_send()

    @pl.loop(1, NZ)
    def _(i):
        for g in (1, 2, 3):
            for from_half in range(2):
                send_rest(g, i, from_half).wait_send()

    for g in range(4):
        swap(g).wait_send()
    for s in (0, 1, 2, 4, 5, 6):
        send_y(s).wait_send()
    for s in range(8):
        for kind in range(6):
            send_x(s, kind).wait_send()

    spread_here(1, 1)
    forward(7)
    spread_here(1, 2)
    forward(6)
    update[...] += expand(0)
    spread_here(1, 3)
    forward(5)
    update[...] += expand(3)
    forward(4)
    for half in range(2):
        for t in (1, 2, 3):
            dir_y(half, t).wait_send()
    for s in (0, 1, 2, 3, 5, 6, 7):
        for kind in range(4):
            dir_x(s, kind).wait_send()
    update[...] += expand(2)
    for kind in range(4):
        dir_x(4, kind).wait_send()


def write_out(a_ref, b_ref, c_ref, a_out, b_out, c_out, sems):
    copies = [
        pltpu.make_async_copy(src, dst, sems.at[i])
        for i, (src, dst) in enumerate(((a_ref, a_out), (b_ref, b_out), (c_ref, c_out)))
    ]
    for copy in copies:
        copy.start()
    for copy in copies:
        copy.wait()


def on_device(gradient, projector, first_moment, second_moment):
    vmem = pl.BlockSpec(memory_space=pltpu.VMEM)
    hbm = pl.BlockSpec(memory_space=pltpu.HBM)
    dma = pltpu.SemaphoreType.DMA
    f32, bf16 = jnp.float32, jnp.bfloat16
    shapes = (
        jax.ShapeDtypeStruct((ROWS, COLS), f32),
        jax.ShapeDtypeStruct((OWN, COLS), f32),
        jax.ShapeDtypeStruct((OWN, COLS), f32),
    )
    results = pl.pallas_call(
        kernel,
        out_shape=shapes,
        in_specs=[hbm] * 4,
        out_specs=(vmem, vmem, vmem),
        scratch_shapes=[
            pltpu.VMEM((ROWS, COLS), bf16),
            pltpu.VMEM((16, 1024), bf16),
            pltpu.VMEM((OWN, COLS), f32),
            pltpu.VMEM((OWN, COLS), f32),
            pltpu.VMEM((4, 16, 2, 16, CHUNK), bf16),
            pltpu.VMEM((8, NX, PART, COLS), f32),
            pltpu.VMEM((8, NX, PART, COLS), bf16),
            pltpu.VMEM((8, 2, HALF, COLS), bf16),
            pltpu.VMEM((8, 6, HALF, COLS), bf16),
            pltpu.VMEM((8, PART, COLS), bf16),
            pltpu.VMEM((8, PART, COLS), bf16),
            pltpu.VMEM((8, NX, PART, COLS), bf16),
            dma((4,)),
            dma((16,)), dma((16,)),
            dma, dma,
            dma((3, 2, NZ)), dma((3, 2, NZ)),
            dma((4,)), dma((4,)),
            dma((8, 6)), dma((8, 6)),
            dma((8,)), dma((8,)),
            dma((8, 4)), dma((8, 4)),
            dma((2, 3)), dma((2, 3)),
        ],
        compiler_params=pltpu.CompilerParams(
            collective_id=0, has_side_effects=True, vmem_limit_bytes=60 * 1024 * 1024
        ),
        cost_estimate=pl.CostEstimate(flops=4 * 512 * 1024 * 896, bytes_accessed=4 << 20, transcendentals=0),
    )(gradient, projector, first_moment, second_moment)
    return pl.pallas_call(
        write_out,
        out_shape=shapes,
        in_specs=[vmem] * 3,
        out_specs=(hbm, hbm, hbm),
        scratch_shapes=[dma((3,))],
    )(*results)


def solution(mesh):
    return jax.shard_map(
        on_device,
        mesh=mesh,
        in_specs=(P("row", "col"), P(("row", "col"), None), P("row", "col"), P("row", "col")),
        out_specs=(P("row", "col"), P("row", "col"), P("row", "col")),
        check_vma=False,
    )
```

```python
import jax
import jax.numpy as jnp
from jax import lax
from jax.experimental import pallas as pl
from jax.experimental.pallas import tpu as pltpu
from jax.sharding import PartitionSpec as P

MESH = pl.DeviceIdType.MESH
beta_first = 0.9
beta_second = 0.999
epsilon = 1e-08

NX, NY, NZ = 4, 4, 8
CHUNK = 256
OWN = 64
PART = 32
HALF = 16
SUM_RELAYED = (0, 1, 2, 3, 4, 5, 6, 7)
DIR_RELAYED = (0, 1, 2, 3, 4, 5, 6, 7)
GROUPS = ((0, 1), (1, 1), (2, 2))
COLS = 896
ROWS = 512


def kernel(
    grad_hbm, proj_hbm, mom1_hbm, mom2_hbm, update, first, second,
    grad, proj, mom1, mom2, pg, part, xs, ss, xr, xd, ys, yr, dirs,
    local_sem, ps_send, ps_recv, hf_send, hf_recv, pf_send, pf_recv, sw_send, sw_recv,
    xs_sem, xr_sem, ys_sem, yr_sem, dx_send, dx_recv, dy_send, dy_recv,
):
    row = lax.axis_index("row")
    col = lax.axis_index("col")
    x, y = lax.rem(row, NX), lax.div(row, NX)
    k, h, z = lax.rem(col, 2), lax.rem(lax.div(col, 2), 2), lax.div(col, 4)
    zh = z * 2 + h

    def at_zh(dz, flip):
        other_z = lax.rem(z + dz, NZ)
        other_h = lax.rem(h + flip, 2)
        return (row, (other_z * 2 + other_h) * 2 + k)

    def x_of(d):
        return lax.rem(x + d, NX)

    def at_x(d):
        return (y * NX + x_of(d), col)

    def y_of(t):
        return lax.rem(lax.div(y, 2) + t // 2, 2) * 2 + lax.rem(lax.rem(y, 2) + t % 2, 2)

    def at_y(t):
        return (y_of(t) * NX + x, col)

    def remote(src, dst, send_sem, recv_sem, device):
        return pltpu.make_async_remote_copy(
            src_ref=src, dst_ref=dst, send_sem=send_sem, recv_sem=recv_sem, device_id=device, device_id_type=MESH)

    def wait_bytes(ref, sem):
        pltpu.make_async_copy(ref, ref, sem).wait()

    other_core = (row, zh * 2 + 1 - k)

    fetch_proj = pltpu.make_async_copy(proj_hbm, proj, local_sem.at[0])
    fetch_grad = pltpu.make_async_copy(grad_hbm, grad, local_sem.at[1])
    fetch_mom1 = pltpu.make_async_copy(mom1_hbm, mom1, local_sem.at[2])
    fetch_mom2 = pltpu.make_async_copy(mom2_hbm, mom2, local_sem.at[3])
    fetch_proj.start()

    barrier = pltpu.get_barrier_semaphore()

    @pl.loop(1, 16)
    def _(i):
        pl.semaphore_signal(barrier, inc=1, device_id=at_zh(lax.div(i, 2), lax.rem(i, 2)), device_id_type=MESH)

    for t in (1, 2, 3):
        pl.semaphore_signal(barrier, inc=1, device_id=at_y(t), device_id_type=MESH)
    for d in (1, 3):
        pl.semaphore_signal(barrier, inc=1, device_id=at_x(d), device_id_type=MESH)
    pl.semaphore_signal(barrier, inc=1, device_id=other_core, device_id_type=MESH)

    fetch_grad.start()
    fetch_mom1.start()
    fetch_mom2.start()
    fetch_proj.wait()

    for j in range(NY):
        owned = proj[:, pl.ds(pl.multiple_of(y_of(3 - j) * CHUNK, CHUNK), CHUNK)]
        for half in range(2):
            s = 4 * half + j
            picked = [owned[:, OWN * i + PART * half : OWN * i + PART * (half + 1)] for i in range(NX)]
            pg[s // 2, zh, k, :, pl.ds(s % 2 * 128, 128)] = jnp.concatenate(picked, axis=1)
    pl.semaphore_wait(barrier, 21)

    def send_first(i):
        piece = pg.at[0, zh, k]
        return remote(piece, piece, ps_send, ps_recv, at_zh(lax.div(i, 2), lax.rem(i, 2)))

    @pl.loop(0, 15)
    def _(i):
        send_first(15 - i).start()

    def send_half():
        piece = pg.at[pl.ds(1, 3), zh, k]
        return remote(piece, piece, hf_send, hf_recv, at_zh(0, 1))

    def send_rest(g, i, from_half):
        piece = pg.at[pl.ds(*GROUPS[g]), z * 2 + lax.rem(h + from_half, 2), k]
        return remote(piece, piece, pf_send, pf_recv.at[g - 1], at_zh(i, 0))

    def send_rests(g, from_half):
        @pl.loop(1, NZ)
        def _(i):
            send_rest(g, lax.rem(i + 3, NZ - 1) + 1, from_half).start()

    def swap(g):
        piece = pg.at[pl.ds(*GROUPS[g]), :, k]
        return remote(piece, piece, sw_send, sw_recv.at[g], other_core)

    send_half().start()
    send_rests(1, 0)
    send_half().wait_recv()
    send_rests(1, 1)
    send_rests(2, 0)
    send_rests(2, 1)

    wait_bytes(pg.at[0, pl.ds(0, 15), 0], ps_recv)
    swap(0).start()
    fetch_grad.wait()
    swap(0).wait_recv()

    def rest_here(g):
        wait_bytes(pg.at[pl.ds(0, GROUPS[g][1]), pl.ds(0, 14), 0], pf_recv.at[g - 1])
        swap(g).start()

    low, high = pl.ds(0, HALF), pl.ds(HALF, HALF)

    def send_x(s, kind):
        if s not in SUM_RELAYED:
            d = (2, 1, 3)[kind]
            return remote(
                xs.at[s, x_of(d)], xd.at[s, kind], xs_sem.at[1], xr_sem.at[s, 0], at_x(d))
        src, d = (
            (xs.at[s, x_of(2), low], 1),
            (xs.at[s, x_of(2), high], 3),
            (xs.at[s, x_of(1), high], 1),
            (xs.at[s, x_of(3), low], 3),
            (ss.at[s, 0], 1),
            (ss.at[s, 1], 3),
        )[kind]
        return remote(src, xr.at[s, kind], xs_sem.at[0], xr_sem.at[s, kind], at_x(d))

    def project(q):
        sums = lax.dot_general(
            pg[q].reshape(ROWS, CHUNK), grad[...], (((0,), (0,)), ((), ())), preferred_element_type=jnp.float32)
        sums = sums.reshape(2, NX, PART, COLS)
        part[pl.ds(2 * q, 2)] = sums
        xs[pl.ds(2 * q, 2)] = sums.astype(jnp.bfloat16)
        for kinds in ((0, 1), (2, 3)):
            for s in (2 * q, 2 * q + 1):
                for kind in kinds:
                    if s in SUM_RELAYED:
                        send_x(s, kind).start()
        for s in (2 * q, 2 * q + 1):
            if s not in SUM_RELAYED:
                for kind in range(3):
                    send_x(s, kind).start()

    def relay(s):
        if s not in SUM_RELAYED:
            return
        send_x(s, 0).wait_recv()
        ss[s, 0] = (part[s, x_of(1), low] + xr[s, 0].astype(jnp.float32)).astype(jnp.bfloat16)
        send_x(s, 4).start()
        send_x(s, 1).wait_recv()
        ss[s, 1] = (part[s, x_of(3), high] + xr[s, 1].astype(jnp.float32)).astype(jnp.bfloat16)
        send_x(s, 5).start()

    def sum_x(s):
        if s not in SUM_RELAYED:
            wait_bytes(xd.at[s], xr_sem.at[s, 0])
            total = part[s, x]
            for kind in range(3):
                total += xd[s, kind].astype(jnp.float32)
            return total
        for kind in range(2, 6):
            send_x(s, kind).wait_recv()
        lower = part[s, x, low] + xr[s, 3].astype(jnp.float32) + xr[s, 4].astype(jnp.float32)
        upper = part[s, x, high] + xr[s, 2].astype(jnp.float32) + xr[s, 5].astype(jnp.float32)
        return jnp.concatenate([lower, upper], axis=0)

    def send_y(s):
        return remote(ys.at[s], yr.at[s], ys_sem, yr_sem.at[s], at_y(3 - s % 4))

    def finish(s):
        ys[s] = sum_x(s).astype(jnp.bfloat16)
        send_y(s).start()

    def dir_y(half, t):
        own = 4 * half + 3
        return remote(dirs.at[own, x], dirs.at[own - t, x], dy_send, dy_recv.at[half, t - 1], at_y(t))

    def dir_x(s, kind):
        if s not in DIR_RELAYED:
            src, d = dirs.at[s, x], (2, 1, 3)[kind]
            return remote(src, src, dx_send, dx_recv.at[s, 0], at_x(d))
        src, d = (
            (dirs.at[s, x], 1),
            (dirs.at[s, x], 3),
            (dirs.at[s, x_of(3), low], 1),
            (dirs.at[s, x_of(1), high], 3),
        )[kind]
        return remote(src, src, dx_send, dx_recv.at[s, kind], at_x(d))

    def spread(s):
        for kind in range(2 if s in DIR_RELAYED else 3):
            dir_x(s, kind).start()

    def spread_here(half, t):
        dir_y(half, t).wait_recv()
        spread(4 * half + 3 - t)

    def forward(s):
        if s not in DIR_RELAYED:
            return
        for kind in range(2):
            dir_x(s, kind).wait_recv()
            dir_x(s, kind + 2).start()

    def expand(q):
        for s in (2 * q, 2 * q + 1):
            if s in DIR_RELAYED:
                for kind in range(2, 4):
                    dir_x(s, kind).wait_recv()
            else:
                wait_bytes(dirs.at[s, pl.ds(0, 3)], dx_recv.at[s, 0])
        return jnp.dot(
            pg[q].reshape(ROWS, CHUNK), dirs[pl.ds(2 * q, 2)].reshape(CHUNK, COLS), preferred_element_type=jnp.float32)

    def step(half):
        own = 4 * half + 3
        rows = pl.ds(PART * half, PART)
        lowrank = sum_x(own)
        for j in range(3):
            send_y(4 * half + j).wait_recv()
            lowrank += yr[4 * half + j].astype(jnp.float32)
        first_new = beta_first * mom1[rows] + (1.0 - beta_first) * lowrank
        second_new = beta_second * mom2[rows] + (1.0 - beta_second) * lowrank * lowrank
        dirs[own, x] = (first_new / (jnp.sqrt(second_new) + epsilon)).astype(jnp.bfloat16)
        for t in (1, 2, 3):
            dir_y(half, t).start()
        spread(own)
        first[rows] = first_new
        second[rows] = second_new

    project(0)
    rest_here(1)
    relay(0)
    relay(1)
    swap(1).wait_recv()
    project(1)
    finish(0)
    finish(1)
    rest_here(2)
    relay(2)
    relay(3)
    swap(2).wait_recv()
    project(2)
    project(3)
    finish(2)
    fetch_mom1.wait()
    fetch_mom2.wait()
    relay(4)
    relay(5)
    step(0)
    relay(6)
    relay(7)
    finish(4)
    finish(5)
    spread_here(0, 1)
    finish(6)
    forward(3)
    spread_here(0, 2)
    step(1)
    spread_here(0, 3)
    forward(2)
    forward(1)
    spread_here(1, 1)
    forward(0)
    forward(7)
    spread_here(1, 2)
    update[...] = expand(1)
    spread_here(1, 3)
    forward(6)
    forward(5)
    update[...] += expand(0)
    forward(4)
    update[...] += expand(3)
    update[...] += expand(2)

    wait_bytes(pg.at[0, pl.ds(0, 15), 0], ps_send)
    send_half().wait_send()
    wait_bytes(pg.at[pl.ds(0, 3), pl.ds(0, 14), 0], pf_send)
    wait_bytes(pg.at[:, :, 0], sw_send)
    wait_bytes(ys.at[pl.ds(0, 6)], ys_sem)
    if SUM_RELAYED:
        wait_bytes(xr.at[pl.ds(0, len(SUM_RELAYED))], xs_sem.at[0])
    if len(SUM_RELAYED) < 8:
        wait_bytes(xd.at[pl.ds(0, 8 - len(SUM_RELAYED))], xs_sem.at[1])
    wait_bytes(dirs.at[pl.ds(0, 2), pl.ds(0, 3)], dy_send)
    wait_bytes(dirs.at[:, pl.ds(0, 3)], dx_send)


def write_out(a_ref, b_ref, c_ref, a_out, b_out, c_out, sems):
    copies = [
        pltpu.make_async_copy(src, dst, sems.at[i])
        for i, (src, dst) in enumerate(((a_ref, a_out), (b_ref, b_out), (c_ref, c_out)))
    ]
    for copy in copies:
        copy.start()
    for copy in copies:
        copy.wait()


def on_device(gradient, projector, first_moment, second_moment):
    vmem = pl.BlockSpec(memory_space=pltpu.VMEM)
    hbm = pl.BlockSpec(memory_space=pltpu.HBM)
    dma = pltpu.SemaphoreType.DMA
    f32, bf16 = jnp.float32, jnp.bfloat16
    shapes = (
        jax.ShapeDtypeStruct((ROWS, COLS), f32),
        jax.ShapeDtypeStruct((OWN, COLS), f32),
        jax.ShapeDtypeStruct((OWN, COLS), f32),
    )
    results = pl.pallas_call(
        kernel,
        out_shape=shapes,
        in_specs=[hbm] * 4,
        out_specs=(vmem, vmem, vmem),
        scratch_shapes=[
            pltpu.VMEM((ROWS, COLS), bf16),
            pltpu.VMEM((16, 1024), bf16),
            pltpu.VMEM((OWN, COLS), f32),
            pltpu.VMEM((OWN, COLS), f32),
            pltpu.VMEM((4, 16, 2, 16, CHUNK), bf16),
            pltpu.VMEM((8, NX, PART, COLS), f32),
            pltpu.VMEM((8, NX, PART, COLS), bf16),
            pltpu.VMEM((8, 2, HALF, COLS), bf16),
            pltpu.VMEM((8, 6, HALF, COLS), bf16),
            pltpu.VMEM((8, 3, PART, COLS), bf16),
            pltpu.VMEM((8, PART, COLS), bf16),
            pltpu.VMEM((8, PART, COLS), bf16),
            pltpu.VMEM((8, NX, PART, COLS), bf16),
            dma((4,)),
            dma, dma,
            dma, dma,
            dma, dma((2,)),
            dma, dma((3,)),
            dma((2,)), dma((8, 6)),
            dma, dma((8,)),
            dma, dma((8, 4)),
            dma, dma((2, 3)),
        ],
        compiler_params=pltpu.CompilerParams(
            collective_id=0, has_side_effects=True, vmem_limit_bytes=40 * 1024 * 1024
        ),
        cost_estimate=pl.CostEstimate(flops=4 * 512 * 1024 * 896, bytes_accessed=4 << 20, transcendentals=0),
    )(*[pltpu.with_memory_space_constraint(a, pltpu.HBM) for a in (gradient, projector, first_moment, second_moment)])
    return pl.pallas_call(
        write_out,
        out_shape=shapes,
        in_specs=[vmem] * 3,
        out_specs=(hbm, hbm, hbm),
        scratch_shapes=[dma((3,))],
        compiler_params=pltpu.CompilerParams(vmem_limit_bytes=8 * 1024 * 1024),
    )(*results)


def solution(mesh):
    return jax.shard_map(
        on_device,
        mesh=mesh,
        in_specs=(P("row", "col"), P(("row", "col"), None), P("row", "col"), P("row", "col")),
        out_specs=(P("row", "col"), P("row", "col"), P("row", "col")),
        check_vma=False,
    )
```

```python
import jax
import jax.numpy as jnp
from jax import lax
from jax.experimental import pallas as pl
from jax.experimental.pallas import tpu as pltpu
from jax.sharding import PartitionSpec as P

MESH = pl.DeviceIdType.MESH
beta_first = 0.9
beta_second = 0.999
epsilon = 1e-08

NX, NY, NZ = 4, 4, 8
CHUNK = 256
OWN = 64
PART = 32
HALF = 16
SUM_RELAYED = (0, 1, 2, 3, 4, 5, 6, 7)
DIR_RELAYED = (0, 1, 2, 3, 4, 5, 6, 7)
GROUPS = ((0, 1), (1, 1), (2, 2))
COLS = 896
ROWS = 512


def kernel(
    grad_hbm, proj_hbm, mom1_hbm, mom2_hbm, update, first, second,
    grad, proj, mom1, mom2, pg, part, xs, ss, xr, xd, ys, yr, dirs,
    local_sem, ps_send, ps_recv, hf_send, hf_recv, pf_send, pf_recv, sw_send, sw_recv,
    xs_sem, xr_sem, ys_sem, yr_sem, dx_send, dx_recv, dy_send, dy_recv,
):
    row = lax.axis_index("row")
    col = lax.axis_index("col")
    x, y = lax.rem(row, NX), lax.div(row, NX)
    k, h, z = lax.rem(col, 2), lax.rem(lax.div(col, 2), 2), lax.div(col, 4)
    zh = z * 2 + h

    def at_zh(dz, flip):
        other_z = lax.rem(z + dz, NZ)
        other_h = lax.rem(h + flip, 2)
        return (row, (other_z * 2 + other_h) * 2 + k)

    def x_of(d):
        return lax.rem(x + d, NX)

    def at_x(d):
        return (y * NX + x_of(d), col)

    def y_of(t):
        return lax.rem(lax.div(y, 2) + t // 2, 2) * 2 + lax.rem(lax.rem(y, 2) + t % 2, 2)

    def at_y(t):
        return (y_of(t) * NX + x, col)

    def remote(src, dst, send_sem, recv_sem, device):
        return pltpu.make_async_remote_copy(
            src_ref=src, dst_ref=dst, send_sem=send_sem, recv_sem=recv_sem, device_id=device, device_id_type=MESH)

    def wait_bytes(ref, sem):
        pltpu.make_async_copy(ref, ref, sem).wait()

    other_core = (row, zh * 2 + 1 - k)

    fetch_proj = pltpu.make_async_copy(proj_hbm, proj, local_sem.at[0])
    fetch_grad = pltpu.make_async_copy(grad_hbm, grad, local_sem.at[1])
    fetch_mom1 = pltpu.make_async_copy(mom1_hbm, mom1, local_sem.at[2])
    fetch_mom2 = pltpu.make_async_copy(mom2_hbm, mom2, local_sem.at[3])
    fetch_proj.start()

    barrier = pltpu.get_barrier_semaphore()

    @pl.loop(1, 16)
    def _(i):
        pl.semaphore_signal(barrier, inc=1, device_id=at_zh(lax.div(i, 2), lax.rem(i, 2)), device_id_type=MESH)

    for t in (1, 2, 3):
        pl.semaphore_signal(barrier, inc=1, device_id=at_y(t), device_id_type=MESH)
    for d in (1, 3):
        pl.semaphore_signal(barrier, inc=1, device_id=at_x(d), device_id_type=MESH)
    pl.semaphore_signal(barrier, inc=1, device_id=other_core, device_id_type=MESH)

    fetch_grad.start()
    fetch_mom1.start()
    fetch_mom2.start()
    fetch_proj.wait()

    for j in range(NY):
        owned = proj[:, pl.ds(pl.multiple_of(y_of(3 - j) * CHUNK, CHUNK), CHUNK)]
        for half in range(2):
            s = 4 * half + j
            picked = [owned[:, OWN * i + PART * half : OWN * i + PART * (half + 1)] for i in range(NX)]
            pg[s // 2, zh, k, :, pl.ds(s % 2 * 128, 128)] = jnp.concatenate(picked, axis=1)
    pl.semaphore_wait(barrier, 21)

    def send_first(i):
        piece = pg.at[0, zh, k]
        return remote(piece, piece, ps_send, ps_recv, at_zh(lax.div(i, 2), lax.rem(i, 2)))

    @pl.loop(0, 15)
    def _(i):
        send_first(i + 1).start()

    def send_half():
        piece = pg.at[pl.ds(1, 3), zh, k]
        return remote(piece, piece, hf_send, hf_recv, at_zh(0, 1))

    def send_rest(g, i, from_half):
        piece = pg.at[pl.ds(*GROUPS[g]), z * 2 + lax.rem(h + from_half, 2), k]
        return remote(piece, piece, pf_send, pf_recv.at[g - 1], at_zh(i, 0))

    def send_rests(g, from_half):
        @pl.loop(1, NZ)
        def _(i):
            send_rest(g, lax.rem(i + 3, NZ - 1) + 1, from_half).start()

    def swap(g):
        piece = pg.at[pl.ds(*GROUPS[g]), :, k]
        return remote(piece, piece, sw_send, sw_recv.at[g], other_core)

    send_half().start()
    send_rests(1, 0)
    send_half().wait_recv()
    send_rests(1, 1)
    send_rests(2, 0)
    send_rests(2, 1)

    wait_bytes(pg.at[0, pl.ds(0, 15), 0], ps_recv)
    swap(0).start()
    fetch_grad.wait()
    swap(0).wait_recv()

    def rest_here(g):
        wait_bytes(pg.at[pl.ds(0, GROUPS[g][1]), pl.ds(0, 14), 0], pf_recv.at[g - 1])
        swap(g).start()

    low, high = pl.ds(0, HALF), pl.ds(HALF, HALF)

    def send_x(s, kind):
        if s not in SUM_RELAYED:
            d = (2, 1, 3)[kind]
            return remote(
                xs.at[s, x_of(d)], xd.at[s, kind], xs_sem.at[1], xr_sem.at[s, 0], at_x(d))
        src, d = (
            (xs.at[s, x_of(2), low], 1),
            (xs.at[s, x_of(2), high], 3),
            (xs.at[s, x_of(1), high], 1),
            (xs.at[s, x_of(3), low], 3),
            (ss.at[s, 0], 1),
            (ss.at[s, 1], 3),
        )[kind]
        return remote(src, xr.at[s, kind], xs_sem.at[0], xr_sem.at[s, kind], at_x(d))

    def project(q):
        sums = lax.dot_general(
            pg[q].reshape(ROWS, CHUNK), grad[...], (((0,), (0,)), ((), ())), preferred_element_type=jnp.float32)
        sums = sums.reshape(2, NX, PART, COLS)
        part[pl.ds(2 * q, 2)] = sums
        xs[pl.ds(2 * q, 2)] = sums.astype(jnp.bfloat16)
        for kinds in ((0, 1), (2, 3)):
            for s in (2 * q, 2 * q + 1):
                for kind in kinds:
                    if s in SUM_RELAYED:
                        send_x(s, kind).start()
        for s in (2 * q, 2 * q + 1):
            if s not in SUM_RELAYED:
                for kind in range(3):
                    send_x(s, kind).start()

    def relay(s):
        if s not in SUM_RELAYED:
            return
        send_x(s, 0).wait_recv()
        ss[s, 0] = (part[s, x_of(1), low] + xr[s, 0].astype(jnp.float32)).astype(jnp.bfloat16)
        send_x(s, 4).start()
        send_x(s, 1).wait_recv()
        ss[s, 1] = (part[s, x_of(3), high] + xr[s, 1].astype(jnp.float32)).astype(jnp.bfloat16)
        send_x(s, 5).start()

    def sum_x(s):
        if s not in SUM_RELAYED:
            wait_bytes(xd.at[s], xr_sem.at[s, 0])
            total = part[s, x]
            for kind in range(3):
                total += xd[s, kind].astype(jnp.float32)
            return total
        for kind in range(2, 6):
            send_x(s, kind).wait_recv()
        lower = part[s, x, low] + xr[s, 3].astype(jnp.float32) + xr[s, 4].astype(jnp.float32)
        upper = part[s, x, high] + xr[s, 2].astype(jnp.float32) + xr[s, 5].astype(jnp.float32)
        return jnp.concatenate([lower, upper], axis=0)

    def send_y(s):
        return remote(ys.at[s], yr.at[s], ys_sem, yr_sem.at[s], at_y(3 - s % 4))

    def finish(s):
        ys[s] = sum_x(s).astype(jnp.bfloat16)
        send_y(s).start()

    def dir_y(half, t):
        own = 4 * half + 3
        return remote(dirs.at[own, x], dirs.at[own - t, x], dy_send, dy_recv.at[half, t - 1], at_y(t))

    def dir_x(s, kind):
        if s not in DIR_RELAYED:
            src, d = dirs.at[s, x], (2, 1, 3)[kind]
            return remote(src, src, dx_send, dx_recv.at[s, 0], at_x(d))
        src, d = (
            (dirs.at[s, x], 1),
            (dirs.at[s, x], 3),
            (dirs.at[s, x_of(3), low], 1),
            (dirs.at[s, x_of(1), high], 3),
        )[kind]
        return remote(src, src, dx_send, dx_recv.at[s, kind], at_x(d))

    def spread(s):
        for kind in range(2 if s in DIR_RELAYED else 3):
            dir_x(s, kind).start()

    def spread_here(half, t):
        dir_y(half, t).wait_recv()
        spread(4 * half + 3 - t)

    def forward(s):
        if s not in DIR_RELAYED:
            return
        for kind in range(2):
            dir_x(s, kind).wait_recv()
            dir_x(s, kind + 2).start()

    def expand(q):
        for s in (2 * q, 2 * q + 1):
            if s in DIR_RELAYED:
                for kind in range(2, 4):
                    dir_x(s, kind).wait_recv()
            else:
                wait_bytes(dirs.at[s, pl.ds(0, 3)], dx_recv.at[s, 0])
        return jnp.dot(
            pg[q].reshape(ROWS, CHUNK), dirs[pl.ds(2 * q, 2)].reshape(CHUNK, COLS), preferred_element_type=jnp.float32)

    def step(half):
        own = 4 * half + 3
        rows = pl.ds(PART * half, PART)
        lowrank = sum_x(own)
        for j in range(3):
            send_y(4 * half + j).wait_recv()
            lowrank += yr[4 * half + j].astype(jnp.float32)
        first_new = beta_first * mom1[rows] + (1.0 - beta_first) * lowrank
        second_new = beta_second * mom2[rows] + (1.0 - beta_second) * lowrank * lowrank
        dirs[own, x] = (first_new / (jnp.sqrt(second_new) + epsilon)).astype(jnp.bfloat16)
        for t in (1, 2, 3):
            dir_y(half, t).start()
        spread(own)
        first[rows] = first_new
        second[rows] = second_new

    project(0)
    rest_here(1)
    relay(0)
    relay(1)
    swap(1).wait_recv()
    project(1)
    finish(0)
    finish(1)
    rest_here(2)
    relay(2)
    relay(3)
    swap(2).wait_recv()
    project(2)
    project(3)
    finish(2)
    fetch_mom1.wait()
    fetch_mom2.wait()
    relay(4)
    relay(5)
    step(0)
    relay(6)
    relay(7)
    finish(4)
    finish(5)
    spread_here(0, 1)
    finish(6)
    spread_here(0, 2)
    forward(3)
    spread_here(0, 3)
    step(1)
    forward(2)
    forward(1)
    spread_here(1, 1)
    forward(0)
    forward(7)
    spread_here(1, 2)
    spread_here(1, 3)
    update[...] = expand(1)
    forward(6)
    forward(5)
    update[...] += expand(0)
    forward(4)
    update[...] += expand(3)
    update[...] += expand(2)

    wait_bytes(pg.at[0, pl.ds(0, 15), 0], ps_send)
    send_half().wait_send()
    wait_bytes(pg.at[pl.ds(0, 3), pl.ds(0, 14), 0], pf_send)
    wait_bytes(pg.at[:, :, 0], sw_send)
    wait_bytes(ys.at[pl.ds(0, 6)], ys_sem)
    if SUM_RELAYED:
        wait_bytes(xr.at[pl.ds(0, len(SUM_RELAYED))], xs_sem.at[0])
    if len(SUM_RELAYED) < 8:
        wait_bytes(xd.at[pl.ds(0, 8 - len(SUM_RELAYED))], xs_sem.at[1])
    wait_bytes(dirs.at[pl.ds(0, 2), pl.ds(0, 3)], dy_send)
    wait_bytes(dirs.at[:, pl.ds(0, 3)], dx_send)


def write_out(a_ref, b_ref, c_ref, a_out, b_out, c_out, sems):
    copies = [
        pltpu.make_async_copy(src, dst, sems.at[i])
        for i, (src, dst) in enumerate(((a_ref, a_out), (b_ref, b_out), (c_ref, c_out)))
    ]
    for copy in copies:
        copy.start()
    for copy in copies:
        copy.wait()


def on_device(gradient, projector, first_moment, second_moment):
    vmem = pl.BlockSpec(memory_space=pltpu.VMEM)
    hbm = pl.BlockSpec(memory_space=pltpu.HBM)
    dma = pltpu.SemaphoreType.DMA
    f32, bf16 = jnp.float32, jnp.bfloat16
    shapes = (
        jax.ShapeDtypeStruct((ROWS, COLS), f32),
        jax.ShapeDtypeStruct((OWN, COLS), f32),
        jax.ShapeDtypeStruct((OWN, COLS), f32),
    )
    results = pl.pallas_call(
        kernel,
        out_shape=shapes,
        in_specs=[hbm] * 4,
        out_specs=(vmem, vmem, vmem),
        scratch_shapes=[
            pltpu.VMEM((ROWS, COLS), bf16),
            pltpu.VMEM((16, 1024), bf16),
            pltpu.VMEM((OWN, COLS), f32),
            pltpu.VMEM((OWN, COLS), f32),
            pltpu.VMEM((4, 16, 2, 16, CHUNK), bf16),
            pltpu.VMEM((8, NX, PART, COLS), f32),
            pltpu.VMEM((8, NX, PART, COLS), bf16),
            pltpu.VMEM((8, 2, HALF, COLS), bf16),
            pltpu.VMEM((8, 6, HALF, COLS), bf16),
            pltpu.VMEM((8, 3, PART, COLS), bf16),
            pltpu.VMEM((8, PART, COLS), bf16),
            pltpu.VMEM((8, PART, COLS), bf16),
            pltpu.VMEM((8, NX, PART, COLS), bf16),
            dma((4,)),
            dma, dma,
            dma, dma,
            dma, dma((2,)),
            dma, dma((3,)),
            dma((2,)), dma((8, 6)),
            dma, dma((8,)),
            dma, dma((8, 4)),
            dma, dma((2, 3)),
        ],
        compiler_params=pltpu.CompilerParams(
            collective_id=0, has_side_effects=True, vmem_limit_bytes=40 * 1024 * 1024
        ),
        cost_estimate=pl.CostEstimate(flops=4 * 512 * 1024 * 896, bytes_accessed=4 << 20, transcendentals=0),
    )(*[pltpu.with_memory_space_constraint(a, pltpu.HBM) for a in (gradient, projector, first_moment, second_moment)])
    return pl.pallas_call(
        write_out,
        out_shape=shapes,
        in_specs=[vmem] * 3,
        out_specs=(hbm, hbm, hbm),
        scratch_shapes=[dma((3,))],
        compiler_params=pltpu.CompilerParams(vmem_limit_bytes=8 * 1024 * 1024),
    )(*results)


def solution(mesh):
    return jax.shard_map(
        on_device,
        mesh=mesh,
        in_specs=(P("row", "col"), P(("row", "col"), None), P("row", "col"), P("row", "col")),
        out_specs=(P("row", "col"), P("row", "col"), P("row", "col")),
        check_vma=False,
    )
```

```python
import jax
import jax.numpy as jnp
from jax import lax
from jax.experimental import pallas as pl
from jax.experimental.pallas import tpu as pltpu
from jax.sharding import PartitionSpec as P

MESH = pl.DeviceIdType.MESH
beta_first = 0.9
beta_second = 0.999
epsilon = 1e-08

NX, NY, NZ = 4, 4, 8
CHUNK = 256
OWN = 64
PART = 32
HALF = 16
SUM_RELAYED = (0, 1, 2, 3, 4, 5, 6, 7)
DIR_RELAYED = (0, 1, 2, 3, 4, 5, 6, 7)
GROUPS = ((0, 1), (1, 1), (2, 2))
COLS = 896
ROWS = 512


def kernel(
    grad_hbm, proj_hbm, mom1_hbm, mom2_hbm, update, first, second,
    grad, proj, mom1, mom2, pg, part, xs, ss, xr, xd, ys, yr, dirs,
    local_sem, ps_send, ps_recv, hf_send, hf_recv, pf_send, pf_recv, sw_send, sw_recv,
    xs_sem, xr_sem, ys_sem, yr_sem, dx_send, dx_recv, dy_send, dy_recv,
):
    row = lax.axis_index("row")
    col = lax.axis_index("col")
    x, y = lax.rem(row, NX), lax.div(row, NX)
    k, h, z = lax.rem(col, 2), lax.rem(lax.div(col, 2), 2), lax.div(col, 4)
    zh = z * 2 + h

    def at_zh(dz, flip):
        other_z = lax.rem(z + dz, NZ)
        other_h = lax.rem(h + flip, 2)
        return (row, (other_z * 2 + other_h) * 2 + k)

    def x_of(d):
        return lax.rem(x + d, NX)

    def at_x(d):
        return (y * NX + x_of(d), col)

    def y_of(t):
        return lax.rem(lax.div(y, 2) + t // 2, 2) * 2 + lax.rem(lax.rem(y, 2) + t % 2, 2)

    def at_y(t):
        return (y_of(t) * NX + x, col)

    def remote(src, dst, send_sem, recv_sem, device):
        return pltpu.make_async_remote_copy(
            src_ref=src, dst_ref=dst, send_sem=send_sem, recv_sem=recv_sem, device_id=device, device_id_type=MESH)

    def wait_bytes(ref, sem):
        pltpu.make_async_copy(ref, ref, sem).wait()

    other_core = (row, zh * 2 + 1 - k)

    fetch_proj = pltpu.make_async_copy(proj_hbm, proj, local_sem.at[0])
    fetch_grad = pltpu.make_async_copy(grad_hbm, grad, local_sem.at[1])
    fetch_mom1 = pltpu.make_async_copy(mom1_hbm, mom1, local_sem.at[2])
    fetch_mom2 = pltpu.make_async_copy(mom2_hbm, mom2, local_sem.at[3])
    fetch_proj.start()

    barrier = pltpu.get_barrier_semaphore()

    @pl.loop(1, 16)
    def _(i):
        pl.semaphore_signal(barrier, inc=1, device_id=at_zh(lax.div(i, 2), lax.rem(i, 2)), device_id_type=MESH)

    for t in (1, 2, 3):
        pl.semaphore_signal(barrier, inc=1, device_id=at_y(t), device_id_type=MESH)
    for d in (1, 3):
        pl.semaphore_signal(barrier, inc=1, device_id=at_x(d), device_id_type=MESH)
    pl.semaphore_signal(barrier, inc=1, device_id=other_core, device_id_type=MESH)

    fetch_grad.start()
    fetch_mom1.start()
    fetch_mom2.start()
    fetch_proj.wait()

    for j in range(NY):
        owned = proj[:, pl.ds(pl.multiple_of(y_of(3 - j) * CHUNK, CHUNK), CHUNK)]
        for half in range(2):
            s = 4 * half + j
            picked = [owned[:, OWN * i + PART * half : OWN * i + PART * (half + 1)] for i in range(NX)]
            pg[s // 2, zh, k, :, pl.ds(s % 2 * 128, 128)] = jnp.concatenate(picked, axis=1)
    pl.semaphore_wait(barrier, 21)

    def send_first(i):
        piece = pg.at[0, zh, k]
        return remote(piece, piece, ps_send, ps_recv, at_zh(lax.div(i, 2), lax.rem(i, 2)))

    @pl.loop(0, 15)
    def _(i):
        send_first(i + 1).start()

    def send_half():
        piece = pg.at[pl.ds(1, 3), zh, k]
        return remote(piece, piece, hf_send, hf_recv, at_zh(0, 1))

    def send_rest(g, i, from_half):
        piece = pg.at[pl.ds(*GROUPS[g]), z * 2 + lax.rem(h + from_half, 2), k]
        return remote(piece, piece, pf_send, pf_recv.at[g - 1], at_zh(i, 0))

    def send_rests(g, from_half):
        @pl.loop(1, NZ)
        def _(i):
            send_rest(g, lax.rem(i + 3, NZ - 1) + 1, from_half).start()

    def swap(g):
        piece = pg.at[pl.ds(*GROUPS[g]), :, k]
        return remote(piece, piece, sw_send, sw_recv.at[g], other_core)

    send_half().start()
    send_rests(1, 0)
    send_half().wait_recv()
    send_rests(1, 1)

    wait_bytes(pg.at[0, pl.ds(0, 15), 0], ps_recv)
    swap(0).start()
    send_rests(2, 0)
    fetch_grad.wait()
    swap(0).wait_recv()

    def rest_here(g):
        wait_bytes(pg.at[pl.ds(0, GROUPS[g][1]), pl.ds(0, 14), 0], pf_recv.at[g - 1])
        swap(g).start()

    low, high = pl.ds(0, HALF), pl.ds(HALF, HALF)

    def send_x(s, kind):
        if s not in SUM_RELAYED:
            d = (2, 1, 3)[kind]
            return remote(
                xs.at[s, x_of(d)], xd.at[s, kind], xs_sem.at[1], xr_sem.at[s, 0], at_x(d))
        src, d = (
            (xs.at[s, x_of(2), low], 1),
            (xs.at[s, x_of(2), high], 3),
            (xs.at[s, x_of(1), high], 1),
            (xs.at[s, x_of(3), low], 3),
            (ss.at[s, 0], 1),
            (ss.at[s, 1], 3),
        )[kind]
        return remote(src, xr.at[s, kind], xs_sem.at[0], xr_sem.at[s, kind], at_x(d))

    def project(q):
        sums = lax.dot_general(
            pg[q].reshape(ROWS, CHUNK), grad[...], (((0,), (0,)), ((), ())), preferred_element_type=jnp.float32)
        sums = sums.reshape(2, NX, PART, COLS)
        part[pl.ds(2 * q, 2)] = sums
        xs[pl.ds(2 * q, 2)] = sums.astype(jnp.bfloat16)
        for kinds in ((0, 1), (2, 3)):
            for s in (2 * q, 2 * q + 1):
                for kind in kinds:
                    if s in SUM_RELAYED:
                        send_x(s, kind).start()
        for s in (2 * q, 2 * q + 1):
            if s not in SUM_RELAYED:
                for kind in range(3):
                    send_x(s, kind).start()

    def relay(s):
        if s not in SUM_RELAYED:
            return
        send_x(s, 0).wait_recv()
        ss[s, 0] = (part[s, x_of(1), low] + xr[s, 0].astype(jnp.float32)).astype(jnp.bfloat16)
        send_x(s, 4).start()
        send_x(s, 1).wait_recv()
        ss[s, 1] = (part[s, x_of(3), high] + xr[s, 1].astype(jnp.float32)).astype(jnp.bfloat16)
        send_x(s, 5).start()

    def sum_x(s):
        if s not in SUM_RELAYED:
            wait_bytes(xd.at[s], xr_sem.at[s, 0])
            total = part[s, x]
            for kind in range(3):
                total += xd[s, kind].astype(jnp.float32)
            return total
        for kind in range(2, 6):
            send_x(s, kind).wait_recv()
        lower = part[s, x, low] + xr[s, 3].astype(jnp.float32) + xr[s, 4].astype(jnp.float32)
        upper = part[s, x, high] + xr[s, 2].astype(jnp.float32) + xr[s, 5].astype(jnp.float32)
        return jnp.concatenate([lower, upper], axis=0)

    def send_y(s):
        return remote(ys.at[s], yr.at[s], ys_sem, yr_sem.at[s], at_y(3 - s % 4))

    def finish(s):
        ys[s] = sum_x(s).astype(jnp.bfloat16)
        send_y(s).start()

    def dir_y(half, t):
        own = 4 * half + 3
        return remote(dirs.at[own, x], dirs.at[own - t, x], dy_send, dy_recv.at[half, t - 1], at_y(t))

    def dir_x(s, kind):
        if s not in DIR_RELAYED:
            src, d = dirs.at[s, x], (2, 1, 3)[kind]
            return remote(src, src, dx_send, dx_recv.at[s, 0], at_x(d))
        src, d = (
            (dirs.at[s, x], 1),
            (dirs.at[s, x], 3),
            (dirs.at[s, x_of(3), low], 1),
            (dirs.at[s, x_of(1), high], 3),
        )[kind]
        return remote(src, src, dx_send, dx_recv.at[s, kind], at_x(d))

    def spread(s):
        for kind in range(2 if s in DIR_RELAYED else 3):
            dir_x(s, kind).start()

    def spread_here(half, t):
        dir_y(half, t).wait_recv()
        spread(4 * half + 3 - t)

    def forward(s):
        if s not in DIR_RELAYED:
            return
        for kind in range(2):
            dir_x(s, kind).wait_recv()
            dir_x(s, kind + 2).start()

    def expand(q):
        for s in (2 * q, 2 * q + 1):
            if s in DIR_RELAYED:
                for kind in range(2, 4):
                    dir_x(s, kind).wait_recv()
            else:
                wait_bytes(dirs.at[s, pl.ds(0, 3)], dx_recv.at[s, 0])
        return jnp.dot(
            pg[q].reshape(ROWS, CHUNK), dirs[pl.ds(2 * q, 2)].reshape(CHUNK, COLS), preferred_element_type=jnp.float32)

    def step(half):
        own = 4 * half + 3
        rows = pl.ds(PART * half, PART)
        lowrank = sum_x(own)
        for j in range(3):
            send_y(4 * half + j).wait_recv()
            lowrank += yr[4 * half + j].astype(jnp.float32)
        first_new = beta_first * mom1[rows] + (1.0 - beta_first) * lowrank
        second_new = beta_second * mom2[rows] + (1.0 - beta_second) * lowrank * lowrank
        dirs[own, x] = (first_new / (jnp.sqrt(second_new) + epsilon)).astype(jnp.bfloat16)
        for t in (1, 2, 3):
            dir_y(half, t).start()
        spread(own)
        first[rows] = first_new
        second[rows] = second_new

    project(0)
    send_rests(2, 1)
    rest_here(1)
    relay(0)
    relay(1)
    swap(1).wait_recv()
    project(1)
    finish(0)
    finish(1)
    rest_here(2)
    relay(2)
    relay(3)
    swap(2).wait_recv()
    project(2)
    project(3)
    finish(2)
    fetch_mom1.wait()
    fetch_mom2.wait()
    relay(4)
    relay(5)
    step(0)
    relay(6)
    relay(7)
    finish(4)
    spread_here(0, 1)
    finish(5)
    finish(6)
    spread_here(0, 2)
    forward(3)
    spread_here(0, 3)
    step(1)
    forward(2)
    forward(1)
    spread_here(1, 1)
    forward(0)
    forward(7)
    spread_here(1, 2)
    spread_here(1, 3)
    update[...] = expand(1)
    forward(6)
    forward(5)
    update[...] += expand(0)
    forward(4)
    update[...] += expand(3)

    wait_bytes(pg.at[0, pl.ds(0, 15), 0], ps_send)
    send_half().wait_send()
    wait_bytes(pg.at[pl.ds(0, 3), pl.ds(0, 14), 0], pf_send)
    wait_bytes(pg.at[:, :, 0], sw_send)
    wait_bytes(ys.at[pl.ds(0, 6)], ys_sem)
    if SUM_RELAYED:
        wait_bytes(xr.at[pl.ds(0, len(SUM_RELAYED))], xs_sem.at[0])
    if len(SUM_RELAYED) < 8:
        wait_bytes(xd.at[pl.ds(0, 8 - len(SUM_RELAYED))], xs_sem.at[1])
    wait_bytes(dirs.at[pl.ds(0, 2), pl.ds(0, 3)], dy_send)
    wait_bytes(dirs.at[:, pl.ds(0, 3)], dx_send)
    update[...] += expand(2)


def write_out(a_ref, b_ref, c_ref, a_out, b_out, c_out, sems):
    copies = [
        pltpu.make_async_copy(src, dst, sems.at[i])
        for i, (src, dst) in enumerate(((a_ref, a_out), (b_ref, b_out), (c_ref, c_out)))
    ]
    for copy in copies:
        copy.start()
    for copy in copies:
        copy.wait()


def on_device(gradient, projector, first_moment, second_moment):
    vmem = pl.BlockSpec(memory_space=pltpu.VMEM)
    hbm = pl.BlockSpec(memory_space=pltpu.HBM)
    dma = pltpu.SemaphoreType.DMA
    f32, bf16 = jnp.float32, jnp.bfloat16
    shapes = (
        jax.ShapeDtypeStruct((ROWS, COLS), f32),
        jax.ShapeDtypeStruct((OWN, COLS), f32),
        jax.ShapeDtypeStruct((OWN, COLS), f32),
    )
    results = pl.pallas_call(
        kernel,
        out_shape=shapes,
        in_specs=[hbm] * 4,
        out_specs=(vmem, vmem, vmem),
        scratch_shapes=[
            pltpu.VMEM((ROWS, COLS), bf16),
            pltpu.VMEM((16, 1024), bf16),
            pltpu.VMEM((OWN, COLS), f32),
            pltpu.VMEM((OWN, COLS), f32),
            pltpu.VMEM((4, 16, 2, 16, CHUNK), bf16),
            pltpu.VMEM((8, NX, PART, COLS), f32),
            pltpu.VMEM((8, NX, PART, COLS), bf16),
            pltpu.VMEM((8, 2, HALF, COLS), bf16),
            pltpu.VMEM((8, 6, HALF, COLS), bf16),
            pltpu.VMEM((8, 3, PART, COLS), bf16),
            pltpu.VMEM((8, PART, COLS), bf16),
            pltpu.VMEM((8, PART, COLS), bf16),
            pltpu.VMEM((8, NX, PART, COLS), bf16),
            dma((4,)),
            dma, dma,
            dma, dma,
            dma, dma((2,)),
            dma, dma((3,)),
            dma((2,)), dma((8, 6)),
            dma, dma((8,)),
            dma, dma((8, 4)),
            dma, dma((2, 3)),
        ],
        compiler_params=pltpu.CompilerParams(
            collective_id=0, has_side_effects=True, vmem_limit_bytes=40 * 1024 * 1024
        ),
        cost_estimate=pl.CostEstimate(flops=4 * 512 * 1024 * 896, bytes_accessed=4 << 20, transcendentals=0),
    )(*[pltpu.with_memory_space_constraint(a, pltpu.HBM) for a in (gradient, projector, first_moment, second_moment)])
    return pl.pallas_call(
        write_out,
        out_shape=shapes,
        in_specs=[vmem] * 3,
        out_specs=(hbm, hbm, hbm),
        scratch_shapes=[dma((3,))],
        compiler_params=pltpu.CompilerParams(vmem_limit_bytes=8 * 1024 * 1024),
    )(*results)


def solution(mesh):
    return jax.shard_map(
        on_device,
        mesh=mesh,
        in_specs=(P("row", "col"), P(("row", "col"), None), P("row", "col"), P("row", "col")),
        out_specs=(P("row", "col"), P("row", "col"), P("row", "col")),
        check_vma=False,
    )
```

```python
import jax
import jax.numpy as jnp
from jax import lax
from jax.experimental import pallas as pl
from jax.experimental.pallas import tpu as pltpu
from jax.sharding import PartitionSpec as P

MESH = pl.DeviceIdType.MESH
beta_first = 0.9
beta_second = 0.999
epsilon = 1e-08

NX, NY, NZ = 4, 4, 8
CHUNK = 256
OWN = 64
PART = 32
HALF = 16
SUM_RELAYED = (0, 1, 2, 3, 4, 5, 6, 7)
DIR_RELAYED = (0, 1, 2, 3, 4, 5, 6, 7)
GROUPS = ((0, 1), (1, 1), (2, 2))
COLS = 896
ROWS = 512


def kernel(
    grad_hbm, proj_hbm, mom1_hbm, mom2_hbm, update, first, second,
    grad, proj, mom1, mom2, pg, part, xs, ss, xr, xd, ys, yr, dirs,
    local_sem, ps_send, ps_recv, hf_send, hf_recv, pf_send, pf_recv, sw_send, sw_recv,
    xs_sem, xr_sem, ys_sem, yr_sem, dx_send, dx_recv, dy_send, dy_recv,
):
    row = lax.axis_index("row")
    col = lax.axis_index("col")
    x, y = lax.rem(row, NX), lax.div(row, NX)
    k, h, z = lax.rem(col, 2), lax.rem(lax.div(col, 2), 2), lax.div(col, 4)
    zh = z * 2 + h

    def at_zh(dz, flip):
        other_z = lax.rem(z + dz, NZ)
        other_h = lax.rem(h + flip, 2)
        return (row, (other_z * 2 + other_h) * 2 + k)

    def x_of(d):
        return lax.rem(x + d, NX)

    def at_x(d):
        return (y * NX + x_of(d), col)

    def y_of(t):
        return lax.rem(lax.div(y, 2) + t // 2, 2) * 2 + lax.rem(lax.rem(y, 2) + t % 2, 2)

    def at_y(t):
        return (y_of(t) * NX + x, col)

    def remote(src, dst, send_sem, recv_sem, device):
        return pltpu.make_async_remote_copy(
            src_ref=src, dst_ref=dst, send_sem=send_sem, recv_sem=recv_sem, device_id=device, device_id_type=MESH)

    def wait_bytes(ref, sem):
        pltpu.make_async_copy(ref, ref, sem).wait()

    other_core = (row, zh * 2 + 1 - k)

    fetch_proj = pltpu.make_async_copy(proj_hbm, proj, local_sem.at[0])
    fetch_grad = pltpu.make_async_copy(grad_hbm, grad, local_sem.at[1])
    fetch_mom1 = pltpu.make_async_copy(mom1_hbm, mom1, local_sem.at[2])
    fetch_mom2 = pltpu.make_async_copy(mom2_hbm, mom2, local_sem.at[3])
    fetch_proj.start()

    barrier = pltpu.get_barrier_semaphore()

    @pl.loop(1, 16)
    def _(i):
        pl.semaphore_signal(barrier, inc=1, device_id=at_zh(lax.div(i, 2), lax.rem(i, 2)), device_id_type=MESH)

    for t in (1, 2, 3):
        pl.semaphore_signal(barrier, inc=1, device_id=at_y(t), device_id_type=MESH)
    for d in (1, 3):
        pl.semaphore_signal(barrier, inc=1, device_id=at_x(d), device_id_type=MESH)
    pl.semaphore_signal(barrier, inc=1, device_id=other_core, device_id_type=MESH)

    fetch_grad.start()
    fetch_mom1.start()
    fetch_mom2.start()
    fetch_proj.wait()

    for j in range(NY):
        owned = proj[:, pl.ds(pl.multiple_of(y_of(3 - j) * CHUNK, CHUNK), CHUNK)]
        for half in range(2):
            s = 4 * half + j
            picked = [owned[:, OWN * i + PART * half : OWN * i + PART * (half + 1)] for i in range(NX)]
            pg[s // 2, zh, k, :, pl.ds(s % 2 * 128, 128)] = jnp.concatenate(picked, axis=1)
    pl.semaphore_wait(barrier, 21)

    def send_first(i):
        piece = pg.at[0, zh, k]
        return remote(piece, piece, ps_send, ps_recv, at_zh(lax.div(i, 2), lax.rem(i, 2)))

    @pl.loop(0, 15)
    def _(i):
        send_first(i + 1).start()

    def send_half():
        piece = pg.at[pl.ds(1, 3), zh, k]
        return remote(piece, piece, hf_send, hf_recv, at_zh(0, 1))

    def send_rest(g, i, from_half):
        piece = pg.at[pl.ds(*GROUPS[g]), z * 2 + lax.rem(h + from_half, 2), k]
        return remote(piece, piece, pf_send, pf_recv.at[g - 1], at_zh(i, 0))

    def send_rests(g, from_half):
        @pl.loop(1, NZ)
        def _(i):
            send_rest(g, lax.rem(i + 3, NZ - 1) + 1, from_half).start()

    def swap(g):
        piece = pg.at[pl.ds(*GROUPS[g]), :, k]
        return remote(piece, piece, sw_send, sw_recv.at[g], other_core)

    send_half().start()
    send_rests(1, 0)
    send_half().wait_recv()
    send_rests(1, 1)

    wait_bytes(pg.at[0, pl.ds(0, 15), 0], ps_recv)
    swap(0).start()
    send_rests(2, 0)
    fetch_grad.wait()
    swap(0).wait_recv()

    def rest_here(g):
        wait_bytes(pg.at[pl.ds(0, GROUPS[g][1]), pl.ds(0, 14), 0], pf_recv.at[g - 1])
        swap(g).start()

    low, high = pl.ds(0, HALF), pl.ds(HALF, HALF)

    def send_x(s, kind):
        if s not in SUM_RELAYED:
            d = (2, 1, 3)[kind]
            return remote(
                xs.at[s, x_of(d)], xd.at[s, kind], xs_sem.at[1], xr_sem.at[s, 0], at_x(d))
        src, d = (
            (xs.at[s, x_of(2), low], 1),
            (xs.at[s, x_of(2), high], 3),
            (xs.at[s, x_of(1), high], 1),
            (xs.at[s, x_of(3), low], 3),
            (ss.at[s, 0], 1),
            (ss.at[s, 1], 3),
        )[kind]
        return remote(src, xr.at[s, kind], xs_sem.at[0], xr_sem.at[s, kind], at_x(d))

    def project(q):
        sums = lax.dot_general(
            pg[q].reshape(ROWS, CHUNK), grad[...], (((0,), (0,)), ((), ())), preferred_element_type=jnp.float32)
        sums = sums.reshape(2, NX, PART, COLS)
        part[pl.ds(2 * q, 2)] = sums
        xs[pl.ds(2 * q, 2)] = sums.astype(jnp.bfloat16)
        for kinds in ((0, 1), (2, 3)):
            for s in (2 * q, 2 * q + 1):
                for kind in kinds:
                    if s in SUM_RELAYED:
                        send_x(s, kind).start()
        for s in (2 * q, 2 * q + 1):
            if s not in SUM_RELAYED:
                for kind in range(3):
                    send_x(s, kind).start()

    def relay(s):
        if s not in SUM_RELAYED:
            return
        send_x(s, 0).wait_recv()
        ss[s, 0] = (part[s, x_of(1), low] + xr[s, 0].astype(jnp.float32)).astype(jnp.bfloat16)
        send_x(s, 4).start()
        send_x(s, 1).wait_recv()
        ss[s, 1] = (part[s, x_of(3), high] + xr[s, 1].astype(jnp.float32)).astype(jnp.bfloat16)
        send_x(s, 5).start()

    def sum_x(s):
        if s not in SUM_RELAYED:
            wait_bytes(xd.at[s], xr_sem.at[s, 0])
            total = part[s, x]
            for kind in range(3):
                total += xd[s, kind].astype(jnp.float32)
            return total
        for kind in range(2, 6):
            send_x(s, kind).wait_recv()
        lower = part[s, x, low] + xr[s, 3].astype(jnp.float32) + xr[s, 4].astype(jnp.float32)
        upper = part[s, x, high] + xr[s, 2].astype(jnp.float32) + xr[s, 5].astype(jnp.float32)
        return jnp.concatenate([lower, upper], axis=0)

    def send_y(s):
        return remote(ys.at[s], yr.at[s], ys_sem, yr_sem.at[s], at_y(3 - s % 4))

    def finish(s):
        ys[s] = sum_x(s).astype(jnp.bfloat16)
        send_y(s).start()

    def dir_y(half, t):
        own = 4 * half + 3
        return remote(dirs.at[own, x], dirs.at[own - t, x], dy_send, dy_recv.at[half, t - 1], at_y(t))

    def dir_x(s, kind):
        if s not in DIR_RELAYED:
            src, d = dirs.at[s, x], (2, 1, 3)[kind]
            return remote(src, src, dx_send, dx_recv.at[s, 0], at_x(d))
        src, d = (
            (dirs.at[s, x], 1),
            (dirs.at[s, x], 3),
            (dirs.at[s, x_of(3), low], 1),
            (dirs.at[s, x_of(1), high], 3),
        )[kind]
        return remote(src, src, dx_send, dx_recv.at[s, kind], at_x(d))

    def spread(s):
        for kind in range(2 if s in DIR_RELAYED else 3):
            dir_x(s, kind).start()

    def spread_here(half, t):
        dir_y(half, t).wait_recv()
        spread(4 * half + 3 - t)

    def forward(s):
        if s not in DIR_RELAYED:
            return
        for kind in range(2):
            dir_x(s, kind).wait_recv()
            dir_x(s, kind + 2).start()

    def expand(q):
        for s in (2 * q, 2 * q + 1):
            if s in DIR_RELAYED:
                for kind in range(2, 4):
                    dir_x(s, kind).wait_recv()
            else:
                wait_bytes(dirs.at[s, pl.ds(0, 3)], dx_recv.at[s, 0])
        return jnp.dot(
            pg[q].reshape(ROWS, CHUNK), dirs[pl.ds(2 * q, 2)].reshape(CHUNK, COLS), preferred_element_type=jnp.float32)

    def step(half):
        own = 4 * half + 3
        rows = pl.ds(PART * half, PART)
        lowrank = sum_x(own)
        for j in range(3):
            send_y(4 * half + j).wait_recv()
            lowrank += yr[4 * half + j].astype(jnp.float32)
        first_new = beta_first * mom1[rows] + (1.0 - beta_first) * lowrank
        second_new = beta_second * mom2[rows] + (1.0 - beta_second) * lowrank * lowrank
        dirs[own, x] = (first_new / (jnp.sqrt(second_new) + epsilon)).astype(jnp.bfloat16)
        for t in (1, 2, 3):
            dir_y(half, t).start()
        spread(own)
        first[rows] = first_new
        second[rows] = second_new

    project(0)
    send_rests(2, 1)
    rest_here(1)
    relay(0)
    relay(1)
    swap(1).wait_recv()
    project(1)
    finish(0)
    finish(1)
    rest_here(2)
    relay(2)
    relay(3)
    swap(2).wait_recv()
    project(2)
    project(3)
    finish(2)
    fetch_mom1.wait()
    fetch_mom2.wait()
    relay(4)
    relay(5)
    step(0)
    relay(6)
    relay(7)
    finish(4)
    spread_here(0, 1)
    finish(5)
    finish(6)
    spread_here(0, 2)
    forward(3)
    spread_here(0, 3)
    step(1)
    forward(2)
    forward(1)
    spread_here(1, 1)
    forward(0)
    forward(7)
    spread_here(1, 2)
    spread_here(1, 3)
    forward(6)
    forward(5)
    update[...] = expand(1)
    forward(4)
    update[...] += expand(0)
    update[...] += expand(3)

    wait_bytes(pg.at[0, pl.ds(0, 15), 0], ps_send)
    send_half().wait_send()
    wait_bytes(pg.at[pl.ds(0, 3), pl.ds(0, 14), 0], pf_send)
    wait_bytes(pg.at[:, :, 0], sw_send)
    wait_bytes(ys.at[pl.ds(0, 6)], ys_sem)
    if SUM_RELAYED:
        wait_bytes(xr.at[pl.ds(0, len(SUM_RELAYED))], xs_sem.at[0])
    if len(SUM_RELAYED) < 8:
        wait_bytes(xd.at[pl.ds(0, 8 - len(SUM_RELAYED))], xs_sem.at[1])
    wait_bytes(dirs.at[pl.ds(0, 2), pl.ds(0, 3)], dy_send)
    wait_bytes(dirs.at[:, pl.ds(0, 3)], dx_send)
    update[...] += expand(2)


def write_out(a_ref, b_ref, c_ref, a_out, b_out, c_out, sems):
    copies = [
        pltpu.make_async_copy(src, dst, sems.at[i])
        for i, (src, dst) in enumerate(((a_ref, a_out), (b_ref, b_out), (c_ref, c_out)))
    ]
    for copy in copies:
        copy.start()
    for copy in copies:
        copy.wait()


def on_device(gradient, projector, first_moment, second_moment):
    vmem = pl.BlockSpec(memory_space=pltpu.VMEM)
    hbm = pl.BlockSpec(memory_space=pltpu.HBM)
    dma = pltpu.SemaphoreType.DMA
    f32, bf16 = jnp.float32, jnp.bfloat16
    shapes = (
        jax.ShapeDtypeStruct((ROWS, COLS), f32),
        jax.ShapeDtypeStruct((OWN, COLS), f32),
        jax.ShapeDtypeStruct((OWN, COLS), f32),
    )
    results = pl.pallas_call(
        kernel,
        out_shape=shapes,
        in_specs=[hbm] * 4,
        out_specs=(vmem, vmem, vmem),
        scratch_shapes=[
            pltpu.VMEM((ROWS, COLS), bf16),
            pltpu.VMEM((16, 1024), bf16),
            pltpu.VMEM((OWN, COLS), f32),
            pltpu.VMEM((OWN, COLS), f32),
            pltpu.VMEM((4, 16, 2, 16, CHUNK), bf16),
            pltpu.VMEM((8, NX, PART, COLS), f32),
            pltpu.VMEM((8, NX, PART, COLS), bf16),
            pltpu.VMEM((8, 2, HALF, COLS), bf16),
            pltpu.VMEM((8, 6, HALF, COLS), bf16),
            pltpu.VMEM((8, 3, PART, COLS), bf16),
            pltpu.VMEM((8, PART, COLS), bf16),
            pltpu.VMEM((8, PART, COLS), bf16),
            pltpu.VMEM((8, NX, PART, COLS), bf16),
            dma((4,)),
            dma, dma,
            dma, dma,
            dma, dma((2,)),
            dma, dma((3,)),
            dma((2,)), dma((8, 6)),
            dma, dma((8,)),
            dma, dma((8, 4)),
            dma, dma((2, 3)),
        ],
        compiler_params=pltpu.CompilerParams(
            collective_id=0, has_side_effects=True, vmem_limit_bytes=40 * 1024 * 1024
        ),
        cost_estimate=pl.CostEstimate(flops=4 * 512 * 1024 * 896, bytes_accessed=4 << 20, transcendentals=0),
    )(*[pltpu.with_memory_space_constraint(a, pltpu.HBM) for a in (gradient, projector, first_moment, second_moment)])
    return pl.pallas_call(
        write_out,
        out_shape=shapes,
        in_specs=[vmem] * 3,
        out_specs=(hbm, hbm, hbm),
        scratch_shapes=[dma((3,))],
        compiler_params=pltpu.CompilerParams(vmem_limit_bytes=8 * 1024 * 1024),
    )(*results)


def solution(mesh):
    return jax.shard_map(
        on_device,
        mesh=mesh,
        in_specs=(P("row", "col"), P(("row", "col"), None), P("row", "col"), P("row", "col")),
        out_specs=(P("row", "col"), P("row", "col"), P("row", "col")),
        check_vma=False,
    )
```
